32 devices in a mesh: groups: 2 (over y), chol: 4 (over z), walk: 2 (over x), spin: 2 (over core).
Axes of the slice: x: 2, y: 2, z: 4, core: 2. Of those that a mesh axis runs over, the one named last changes fastest.
Arguments:
- orbitals: float32 [16, 2, 1400, 150], P(('groups', 'chol', 'walk'), 'spin'), parts along dimension 0, may hold values from -6 to 6
- intersection_inv: float32 [16, 2, 150, 150], P(('groups', 'chol', 'walk'), 'spin'), parts along dimension 0, may hold values from -0.5 to 0.5
- half_chol: bfloat16 [12, 2, 150, 1400], P('chol', 'spin'), may hold values from -0.013671875 to 0.013671875
- slab_chol: bfloat16 [12, 256, 1400], P('chol'), may hold values from -0.15625 to 0.15625
- aux_field: int32 [16, 12], P('groups', 'chol'), parts along dimension 0, may hold values from 0 to 2
Outputs:
- new_slab: float32 [16, 2, 256, 150], P(('groups', 'chol', 'walk'), 'spin'), parts along dimension 0
The draws below stay inside these ranges and needn't reach their ends.
There are 2 independent parts, one for each index of `groups`. The reference program is written for one: setup_inputs(seed, part) draws one part's arguments, and reference() takes and returns one part's arrays. A program takes and returns all parts, laid end to end along the dimension named above; an argument that names none is the same for every part. Nothing has to cross between parts.
All inputs are finite; a program needn't handle non-finite values.
Results may differ from the reference program's by a relative error of at most 0.003.
Values may be sent and summed in bfloat16 or wider, within the bound.
A program may use at most 64 MiB of HBM per device.

```python
import math
import jax
import jax.numpy as jnp
from jax import lax

ORBITALS = 1400
ELEC_SPIN = 150
SLAB = 256
NCHOL = 12
WALKERS = 8


def with_ends(values, stream_key, smallest, high):
    spot = [jax.random.randint(jax.random.fold_in(stream_key, axis), (), 0, length) for axis, length in enumerate(values.shape)]
    widest = values.shape.index(max(values.shape))
    beside = spot[:widest] + [(spot[widest] + 1) % values.shape[widest]] + spot[widest + 1:]
    return values.at[tuple(spot)].set(smallest).at[tuple(beside)].set(high)


def level_of(stream_key, shape, cuts, low, largest):
    loudness, own = 1.0, jax.random.fold_in(stream_key, 6)
    for axis_at, blocks in cuts:
        steps = jnp.exp(jax.random.uniform(jax.random.fold_in(own, axis_at), (blocks,), jnp.float32, low / len(cuts), largest / len(cuts)))
        loudness = loudness * jnp.repeat(steps, shape[axis_at] // blocks).reshape([-1 if axis == axis_at else 1 for axis in range(len(shape))])
    return loudness


def noise(stream_key, dims, width, limit, cuts=(), held_as=jnp.bfloat16):
    loudness = level_of(stream_key, dims, cuts, -0.22, 0.18) if cuts else 1.0
    values = jax.random.normal(stream_key, dims, jnp.float32) * width * loudness
    return jnp.minimum(jnp.maximum(values, -limit), limit).astype(held_as)


def setup_inputs(seed: int = 0, part: int = 0) -> dict:
    streams_of = jax.random.split(jax.random.key(seed), 6)
    part_keys = jax.random.split(jax.random.fold_in(streams_of[5], part), 6)
    return {
        "orbitals": noise(part_keys[0], (WALKERS, 2, ORBITALS, ELEC_SPIN), 1.0, 6.0, ((0, 8), (1, 2)), jnp.float32),
        "intersection_inv": noise(part_keys[1], (WALKERS, 2, ELEC_SPIN, ELEC_SPIN), ELEC_SPIN ** -0.5, 0.5, ((0, 8), (1, 2)), jnp.float32),
        "half_chol": noise(streams_of[2], (NCHOL, 2, ELEC_SPIN, ORBITALS), (ELEC_SPIN * ORBITALS) ** -0.5, 0.013671875, ((0, 4), (1, 2))),
        "slab_chol": noise(streams_of[3], (NCHOL, SLAB, ORBITALS), ORBITALS ** -0.5, 0.15625, ((0, 4),)),
        "aux_field": with_ends(jax.random.randint(part_keys[4], (WALKERS, NCHOL), 0, 3), jax.random.fold_in(part_keys[4], 1), 0, 2).astype(jnp.int32),
    }


root_three = math.sqrt(3.0)

def one_walker(inputs, half_wide, slab_wide):
    orbitals_w, inverse_w, field_w = inputs
    rotated = jnp.einsum('smk,skn->smn', orbitals_w, inverse_w, precision=lax.Precision.HIGHEST).astype(jnp.bfloat16)
    force_bias = jnp.einsum('gsnm,smn->g', half_wide, rotated.astype(jnp.float32), precision=lax.Precision.HIGHEST)
    shifts = root_three * (field_w.astype(jnp.float32) - 1.0) - force_bias
    combined = jnp.einsum('g,grm->rm', shifts, slab_wide, precision=lax.Precision.HIGHEST)
    lowered = lax.optimization_barrier(orbitals_w.astype(jnp.bfloat16)).astype(jnp.float32)
    update = jnp.einsum('rm,smn->srn', combined, lowered, precision=lax.Precision.HIGHEST)
    return orbitals_w[:, :SLAB, :] - update / math.sqrt(NCHOL)

def reference(orbitals, intersection_inv, half_chol, slab_chol, aux_field):
    half_wide = half_chol.astype(jnp.float32)
    slab_wide = slab_chol.astype(jnp.float32)
    return lax.map(lambda inputs: one_walker(inputs, half_wide, slab_wide), (orbitals, intersection_inv, aux_field))
```

```python
import functools
import math

import jax
import jax.numpy as jnp
from jax import lax
from jax.experimental import pallas as pl
from jax.experimental.pallas import tpu as pltpu
from jax.sharding import PartitionSpec as P

MESH = pl.DeviceIdType.MESH
root_three = math.sqrt(3.0)
NT = (((1,), (1,)), ((), ()))


def up_to(value, step):
    return -(-value // step) * step


def kernel(line, walks, orb_hbm, inv_hbm, half_hbm, slab_hbm, aux_ref, out_ref,
           orb, inv, half, slab, buf, invb, item, fbv, fbo, upd, acc, own, load_sem,
           walk_send, walk_recv, inv_send, inv_recv, fb_send, fb_recv, upd_send, upd_recv):
    me = lax.axis_index("chol")
    spin = lax.axis_index("spin")
    wx = lax.axis_index("walk")
    basis, elec = orb.shape
    vectors = half.shape[0]
    rows = slab.shape[1]
    tall = buf.shape[1]
    scale = 1.0 / math.sqrt(vectors * line)

    loads = [pltpu.make_async_copy(src, dst, load_sem.at[i]) for i, (src, dst) in enumerate(
        ((orb_hbm, orb), (inv_hbm, inv), (half_hbm, half), (slab_hbm, slab)))]
    for load in loads:
        load.start()

    barrier = pltpu.get_barrier_semaphore()
    for k in range(1, line):
        pl.semaphore_signal(barrier, inc=1, device_id={"chol": lax.rem(me + k, line)}, device_id_type=MESH)
    pl.semaphore_signal(barrier, inc=1, device_id={"spin": 1 - spin}, device_id_type=MESH)

    loads[0].wait()
    loads[1].wait()
    eye = (lax.broadcasted_iota(jnp.int32, (tall, elec), 0)
           == lax.broadcasted_iota(jnp.int32, (tall, elec), 1)).astype(jnp.bfloat16)
    invb[me] = jnp.dot(eye, inv[...].astype(jnp.bfloat16), preferred_element_type=jnp.float32).astype(jnp.bfloat16)
    wide = buf.shape[2]
    for start in range(0, basis, 256):
        size = min(256, basis - start)
        piece = lax.dot_general(eye, orb[start:start + size, :].astype(jnp.bfloat16), NT,
                                preferred_element_type=jnp.float32).astype(jnp.bfloat16)
        end = min(start + 256, wide)
        if end - start > size:
            piece = jnp.concatenate([piece, jnp.zeros((tall, end - start - size), jnp.bfloat16)], axis=1)
        buf[me, :, start:end] = piece

    pl.semaphore_wait(barrier, line)

    def copies(q, way, to):
        return (
            pltpu.make_async_remote_copy(invb.at[q], invb.at[q], inv_send.at[way, q], inv_recv.at[q],
                                         device_id={"chol": to}, device_id_type=MESH),
            pltpu.make_async_remote_copy(buf.at[q], buf.at[q], walk_send.at[way, q], walk_recv.at[q],
                                         device_id={"chol": to}, device_id_type=MESH),
        )

    def send_up(q):
        @pl.when(me < line - 1)
        def _():
            for copy in copies(q, 0, me + 1):
                copy.start()

    def send_down(q):
        @pl.when(me > 0)
        def _():
            for copy in copies(q, 1, me - 1):
                copy.start()

    def arrive(q):
        for copy in copies(q, 0, lax.rem(me + 1, line)):
            copy.wait_recv()

    def bias_copy(q):
        return pltpu.make_async_remote_copy(fbv.at[q], fbo.at[q], fb_send.at[q], fb_recv.at[q],
                                            device_id={"spin": 1 - spin}, device_id_type=MESH)

    def update_copy(q):
        return pltpu.make_async_remote_copy(upd.at[q], acc.at[me], upd_send.at[q], upd_recv.at[me],
                                            device_id={"chol": q}, device_id_type=MESH)

    def compute(q, slot):
        x = buf[q, :, 0:basis]
        inverse = invb[q].astype(jnp.float32)
        for g in range(vectors):
            met = lax.dot_general(x, half[g], NT, preferred_element_type=jnp.float32)
            part = jnp.sum(jnp.sum(met * inverse, axis=0, keepdims=True), axis=1, keepdims=True)
            fbv[q, g:g + 1, :] = jnp.broadcast_to(part, (1, rows))
        bias_copy(q).start()
        for g in range(vectors):
            item[slot, g] = lax.dot_general(x, slab[g], NT, preferred_element_type=jnp.float32)

    def updated(q, slot):
        bias_copy(q).wait_recv()
        bias = fbv[q] + fbo[q]
        total = None
        for g in range(vectors):
            field = aux_ref[q * walks + wx, g]
            shift = root_three * (field.astype(jnp.float32) - 1.0) - bias[g:g + 1, :]
            term = item[slot, g] * (shift * scale)
            total = term if total is None else total + term
        return total

    send_up(me)
    send_down(me)
    loads[2].wait()
    loads[3].wait()
    fbv[...] = jnp.zeros_like(fbv)
    compute(me, 0)
    own[...] = updated(me, 0)

    def level(d, carry):
        above, below = me + d, me - d

        @pl.when(above < line)
        def _():
            arrive(above)
            send_down(above)

        @pl.when(below >= 0)
        def _():
            arrive(below)
            send_up(below)

        def meet(side, carry):
            q = me + d - 2 * d * side

            @pl.when((q >= 0) & (q < line))
            def _():
                compute(q, side)
            return carry

        def give(side, carry):
            q = me + d - 2 * d * side

            @pl.when((q >= 0) & (q < line))
            def _():
                upd[q] = updated(q, side).astype(jnp.bfloat16)
                update_copy(q).start()
            return carry

        lax.fori_loop(0, 2, meet, 0)
        lax.fori_loop(0, 2, give, 0)
        return carry

    lax.fori_loop(1, line, level, 0)

    total = own[...]
    for k in range(1, line):
        q = lax.rem(me + k, line)
        pltpu.make_async_remote_copy(upd.at[q], acc.at[q], upd_send.at[q], upd_recv.at[q],
                                     device_id={"chol": q}, device_id_type=MESH).wait_recv()
        total = total + acc[q].astype(jnp.float32)
    out_ref[...] = orb[0:rows, :] - jnp.transpose(total)[:, 0:elec]

    def drain(q, carry):
        @pl.when((q <= me) & (me < line - 1))
        def _():
            for copy in copies(q, 0, lax.rem(me + 1, line)):
                copy.wait_send()

        @pl.when((q >= me) & (me > 0))
        def _():
            for copy in copies(q, 1, lax.rem(me + line - 1, line)):
                copy.wait_send()

        bias_copy(q).wait_send()

        @pl.when(q != me)
        def _():
            update_copy(q).wait_send()
        return carry

    lax.fori_loop(0, line, drain, 0)


def body(orbitals, intersection_inv, half_chol, slab_chol, aux_field):
    line = lax.axis_size("chol")
    walks = lax.axis_size("walk")
    basis, elec = orbitals.shape[2:]
    vectors, rows = slab_chol.shape[:2]
    tall, wide = up_to(elec, 32), up_to(basis, 128)
    bf16, f32 = jnp.bfloat16, jnp.float32
    dma = pltpu.SemaphoreType.DMA
    any_spec = pl.BlockSpec(memory_space=pl.ANY)
    out = pl.pallas_call(
        functools.partial(kernel, line, walks),
        out_shape=jax.ShapeDtypeStruct((rows, elec), f32),
        in_specs=[any_spec] * 4 + [pl.BlockSpec(memory_space=pltpu.SMEM)],
        out_specs=pl.BlockSpec(memory_space=pltpu.VMEM),
        scratch_shapes=[
            pltpu.VMEM((basis, elec), f32),
            pltpu.VMEM((elec, elec), f32),
            pltpu.VMEM((vectors, elec, basis), bf16),
            pltpu.VMEM((vectors, rows, basis), bf16),
            pltpu.VMEM((line, tall, wide), bf16),
            pltpu.VMEM((line, tall, elec), bf16),
            pltpu.VMEM((2, vectors, tall, rows), f32),
            pltpu.VMEM((line, up_to(vectors, 8), rows), f32),
            pltpu.VMEM((line, up_to(vectors, 8), rows), f32),
            pltpu.VMEM((line, tall, rows), bf16),
            pltpu.VMEM((line, tall, rows), bf16),
            pltpu.VMEM((tall, rows), f32),
            dma((4,)),
            dma((2, line)), dma((line,)),
            dma((2, line)), dma((line,)),
            dma((line,)), dma((line,)),
            dma((line,)), dma((line,)),
        ],
        compiler_params=pltpu.CompilerParams(
            collective_id=0, has_side_effects=True, vmem_limit_bytes=48 * 1024 * 1024
        ),
    )(orbitals[0, 0], intersection_inv[0, 0], half_chol[:, 0], slab_chol, aux_field)
    return out[None, None]


def solution(mesh):
    placed = (
        P(("groups", "chol", "walk"), "spin", None, None),
        P(("groups", "chol", "walk"), "spin", None, None),
        P("chol", "spin", None, None),
        P("chol", None, None),
        P("groups", "chol"),
    )
    return jax.shard_map(
        body,
        mesh=mesh,
        in_specs=placed,
        out_specs=P(("groups", "chol", "walk"), "spin", None, None),
        check_vma=False,
    )
```

```python
import functools
import math

import jax
import jax.numpy as jnp
from jax import lax
from jax.experimental import pallas as pl
from jax.experimental.pallas import tpu as pltpu
from jax.sharding import PartitionSpec as P

MESH = pl.DeviceIdType.MESH
root_three = math.sqrt(3.0)
NT = (((1,), (1,)), ((), ()))


def up_to(value, step):
    return -(-value // step) * step


def kernel(line, walks, orb_hbm, inv_hbm, half_hbm, slab_hbm, aux_ref, out_hbm,
           orb, inv, half, slab, res, buf, invb, item, fbv, fbo, upd, acc, own, load_sem,
           walk_send, walk_recv, inv_send, inv_recv, fb_send, fb_recv, upd_send, upd_recv):
    me = lax.axis_index("chol")
    spin = lax.axis_index("spin")
    wx = lax.axis_index("walk")
    elec, basis = orb.shape
    vectors = half.shape[0]
    rows = slab.shape[2]
    lanes = invb.shape[2]
    rest = elec - lanes
    tall = buf.shape[1]
    scale = 1.0 / math.sqrt(vectors * line)

    loads = [pltpu.make_async_copy(src, dst, load_sem.at[i]) for i, (src, dst) in enumerate(
        ((orb_hbm.at[:, 0, :], orb), (inv_hbm.at[:, 0, :], inv), (half_hbm, half), (slab_hbm, slab)))]
    for load in loads:
        load.start()

    barrier = pltpu.get_barrier_semaphore()
    for k in range(1, line):
        pl.semaphore_signal(barrier, inc=1, device_id={"chol": lax.rem(me + k, line)}, device_id_type=MESH)
    pl.semaphore_signal(barrier, inc=1, device_id={"spin": 1 - spin}, device_id_type=MESH)

    loads[0].wait()
    loads[1].wait()
    eye = (lax.broadcasted_iota(jnp.int32, (tall, elec), 0)
           == lax.broadcasted_iota(jnp.int32, (tall, elec), 1)).astype(jnp.bfloat16)
    tall_inv = jnp.dot(eye, inv[...].astype(jnp.bfloat16), preferred_element_type=jnp.float32)
    invb[me, 0:tall, :] = tall_inv[:, 0:lanes].astype(jnp.bfloat16)
    side = [tall_inv[at:at + 32, lanes:elec] for at in range(0, tall, 32)]
    side.append(jnp.zeros((32, lanes - rest * len(side)), jnp.float32))
    invb[me, tall:tall + 32, :] = jnp.concatenate(side, axis=1).astype(jnp.bfloat16)
    wide = buf.shape[2]
    full = elec // 16 * 16
    last = basis // 128 * 128
    buf[me, :, last:wide] = jnp.zeros((tall, wide - last), jnp.bfloat16)
    buf[me, 0:full, 0:basis] = orb[0:full, :].astype(jnp.bfloat16)
    buf[me, full:tall, 0:basis] = jnp.dot(
        eye[0:tall - full, 0:elec - full], orb[full:elec, :].astype(jnp.bfloat16),
        preferred_element_type=jnp.float32).astype(jnp.bfloat16)

    pl.semaphore_wait(barrier, line)

    def copies(q, way, to):
        return (
            pltpu.make_async_remote_copy(invb.at[q], invb.at[q], inv_send.at[way, q], inv_recv.at[q],
                                         device_id={"chol": to}, device_id_type=MESH),
            pltpu.make_async_remote_copy(buf.at[q], buf.at[q], walk_send.at[way, q], walk_recv.at[q],
                                         device_id={"chol": to}, device_id_type=MESH),
        )

    def send_up(q):
        @pl.when(me < line - 1)
        def _():
            for copy in copies(q, 0, me + 1):
                copy.start()

    def send_down(q):
        @pl.when(me > 0)
        def _():
            for copy in copies(q, 1, me - 1):
                copy.start()

    def arrive(q):
        for copy in copies(q, 0, lax.rem(me + 1, line)):
            copy.wait_recv()

    def bias_copy(q):
        return pltpu.make_async_remote_copy(fbv.at[q], fbo.at[q], fb_send.at[q], fb_recv.at[q],
                                            device_id={"spin": 1 - spin}, device_id_type=MESH)

    def update_copy(q):
        return pltpu.make_async_remote_copy(upd.at[q], acc.at[me], upd_send.at[q], upd_recv.at[me],
                                            device_id={"chol": q}, device_id_type=MESH)

    def compute(q, slot):
        x = buf[q, :, 0:basis]
        packed = invb[q].astype(jnp.float32)
        for g in range(vectors):
            met = lax.dot_general(x, half[g], NT, preferred_element_type=jnp.float32)
            part = jnp.sum(met[:, 0:lanes] * packed[0:tall, :], axis=0, keepdims=True)
            part = jnp.sum(part, axis=1, keepdims=True)
            for i in range(tall // 32):
                beside = met[32 * i:32 * i + 32, lanes:elec] * packed[tall:, rest * i:rest * i + rest]
                part = part + jnp.sum(jnp.sum(beside, axis=0, keepdims=True), axis=1, keepdims=True)
            fbv[q, g:g + 1, :] = jnp.broadcast_to(part, (1, rows))
        bias_copy(q).start()
        for g in range(vectors):
            item[slot, g] = jnp.dot(x, slab[g], preferred_element_type=jnp.float32)

    def updated(q, slot):
        bias_copy(q).wait_recv()
        bias = fbv[q] + fbo[q]
        total = None
        for g in range(vectors):
            field = aux_ref[g, q * walks + wx]
            shift = root_three * (field.astype(jnp.float32) - 1.0) - bias[g:g + 1, :]
            term = item[slot, g] * (shift * scale)
            total = term if total is None else total + term
        return total

    send_up(me)
    send_down(me)
    loads[2].wait()
    loads[3].wait()
    fbv[...] = jnp.zeros_like(fbv)
    compute(me, 0)
    own[...] = updated(me, 0)

    def level(d, carry):
        above, below = me + d, me - d

        @pl.when(above < line)
        def _():
            arrive(above)
            send_down(above)

        @pl.when(below >= 0)
        def _():
            arrive(below)
            send_up(below)

        def meet(side, carry):
            q = me + d - 2 * d * side

            @pl.when((q >= 0) & (q < line))
            def _():
                compute(q, side)
            return carry

        def give(side, carry):
            q = me + d - 2 * d * side

            @pl.when((q >= 0) & (q < line))
            def _():
                upd[q] = updated(q, side).astype(jnp.bfloat16)
                update_copy(q).start()
            return carry

        lax.fori_loop(0, 2, meet, 0)
        lax.fori_loop(0, 2, give, 0)
        return carry

    lax.fori_loop(1, line, level, 0)

    total = own[...]
    for k in range(1, line):
        q = lax.rem(me + k, line)
        pltpu.make_async_remote_copy(upd.at[q], acc.at[q], upd_send.at[q], upd_recv.at[q],
                                     device_id={"chol": q}, device_id_type=MESH).wait_recv()
        total = total + acc[q].astype(jnp.float32)
    res[...] = orb[:, 0:rows] - total[0:elec, :]
    leave = pltpu.make_async_copy(res, out_hbm.at[:, 0, :], load_sem.at[0])
    leave.start()
    leave.wait()

    def drain(q, carry):
        @pl.when((q <= me) & (me < line - 1))
        def _():
            for copy in copies(q, 0, lax.rem(me + 1, line)):
                copy.wait_send()

        @pl.when((q >= me) & (me > 0))
        def _():
            for copy in copies(q, 1, lax.rem(me + line - 1, line)):
                copy.wait_send()

        bias_copy(q).wait_send()

        @pl.when(q != me)
        def _():
            update_copy(q).wait_send()
        return carry

    lax.fori_loop(0, line, drain, 0)


def body(orbitals, intersection_inv, half_chol, slab_chol, aux_field):
    line = lax.axis_size("chol")
    walks = lax.axis_size("walk")
    basis, elec = orbitals.shape[2:]
    vectors, rows = slab_chol.shape[:2]
    tall, wide = up_to(elec, 32), up_to(basis, 128)
    bf16, f32 = jnp.bfloat16, jnp.float32
    dma = pltpu.SemaphoreType.DMA
    any_spec = pl.BlockSpec(memory_space=pl.ANY)
    out = pl.pallas_call(
        functools.partial(kernel, line, walks),
        out_shape=jax.ShapeDtypeStruct((elec, 1, rows), f32),
        in_specs=[any_spec] * 4 + [pl.BlockSpec(memory_space=pltpu.SMEM)],
        out_specs=any_spec,
        scratch_shapes=[
            pltpu.VMEM((elec, basis), f32),
            pltpu.VMEM((elec, elec), f32),
            pltpu.VMEM((vectors, elec, basis), bf16),
            pltpu.VMEM((vectors, basis, rows), bf16),
            pltpu.VMEM((elec, rows), f32),
            pltpu.VMEM((line, tall, wide), bf16),
            pltpu.VMEM((line, tall + 32, 128), bf16),
            pltpu.VMEM((2, vectors, tall, rows), f32),
            pltpu.VMEM((line, up_to(vectors, 8), rows), f32),
            pltpu.VMEM((line, up_to(vectors, 8), rows), f32),
            pltpu.VMEM((line, tall, rows), bf16),
            pltpu.VMEM((line, tall, rows), bf16),
            pltpu.VMEM((tall, rows), f32),
            dma((4,)),
            dma((2, line)), dma((line,)),
            dma((2, line)), dma((line,)),
            dma((line,)), dma((line,)),
            dma((line,)), dma((line,)),
        ],
        compiler_params=pltpu.CompilerParams(
            collective_id=0, has_side_effects=True, vmem_limit_bytes=63 * 1024 * 1024
        ),
    )(
        jnp.transpose(orbitals[0], (2, 0, 1)), jnp.transpose(intersection_inv[0], (1, 0, 2)),
        half_chol[:, 0], jnp.transpose(slab_chol, (0, 2, 1)), jnp.transpose(aux_field),
    )
    return jnp.transpose(out, (1, 2, 0))[None]


def solution(mesh):
    placed = (
        P(("groups", "chol", "walk"), "spin", None, None),
        P(("groups", "chol", "walk"), "spin", None, None),
        P("chol", "spin", None, None),
        P("chol", None, None),
        P("groups", "chol"),
    )
    return jax.shard_map(
        body,
        mesh=mesh,
        in_specs=placed,
        out_specs=P(("groups", "chol", "walk"), "spin", None, None),
        check_vma=False,
    )
```

```python
import functools
import math

import jax
import jax.numpy as jnp
from jax import lax
from jax.experimental import pallas as pl
from jax.experimental.pallas import tpu as pltpu
from jax.sharding import PartitionSpec as P

MESH = pl.DeviceIdType.MESH
root_three = math.sqrt(3.0)
NT = (((1,), (1,)), ((), ()))


def up_to(value, step):
    return -(-value // step) * step


def kernel(line, walks, orb_hbm, inv_hbm, half_hbm, slab_hbm, aux_ref, out_hbm,
           orb, inv, half, slab, half_end, slab_end, res, buf, invb, item, fbv, fbo, fbe, upd, acc, total, load_sem,
           walk_send, walk_recv, inv_send, inv_recv, fb_send, fb_recv, mate_send, mate_recv, upd_send, upd_recv,
           end_send, end_recv):
    me = lax.axis_index("chol")
    spin = lax.axis_index("spin")
    wx = lax.axis_index("walk")
    elec, basis = orb.shape
    vectors = half.shape[0]
    rows = slab.shape[2]
    lanes = invb.shape[2]
    rest = elec - lanes
    tall, wide = buf.shape[1:]
    cut = basis - slab_end.shape[1]
    scale = 1.0 / math.sqrt(vectors * line)
    is_end = (me == 0) | (me == line - 1)
    is_helper = (me == 1) | (me == line - 2)
    mate = jnp.where(me == 0, 1, jnp.where(me == 1, 0, jnp.where(me == line - 1, line - 2, line - 1)))
    end = jnp.where(is_end, me, mate)

    loads = [pltpu.make_async_copy(src, dst, load_sem.at[i]) for i, (src, dst) in enumerate(
        ((orb_hbm.at[:, 0, :], orb), (inv_hbm.at[:, 0, :], inv), (half_hbm, half), (slab_hbm, slab)))]
    for load in loads:
        load.start()

    barrier = pltpu.get_barrier_semaphore()
    for k in range(1, line):
        pl.semaphore_signal(barrier, inc=1, device_id={"chol": lax.rem(me + k, line)}, device_id_type=MESH)
    pl.semaphore_signal(barrier, inc=1, device_id={"spin": 1 - spin}, device_id_type=MESH)


    @pl.when(is_end | is_helper)
    def _():
        pl.semaphore_signal(barrier, inc=1, device_id={"chol": mate, "spin": 1 - spin}, device_id_type=MESH)

    loads[0].wait()
    loads[1].wait()
    eye = (lax.broadcasted_iota(jnp.int32, (tall, elec), 0)
           == lax.broadcasted_iota(jnp.int32, (tall, elec), 1)).astype(jnp.bfloat16)
    tall_inv = jnp.dot(eye, inv[...].astype(jnp.bfloat16), preferred_element_type=jnp.float32)
    invb[me, 0:tall, :] = tall_inv[:, 0:lanes].astype(jnp.bfloat16)
    side = [tall_inv[at:at + 32, lanes:elec] for at in range(0, tall, 32)]
    side.append(jnp.zeros((32, lanes - rest * len(side)), jnp.float32))
    invb[me, tall:tall + 32, :] = jnp.concatenate(side, axis=1).astype(jnp.bfloat16)
    full = elec // 16 * 16
    last = basis // 128 * 128
    buf[me, :, last:wide] = jnp.zeros((tall, wide - last), jnp.bfloat16)
    buf[me, 0:full, 0:basis] = orb[0:full, :].astype(jnp.bfloat16)
    buf[me, full:tall, 0:basis] = jnp.dot(
        eye[0:tall - full, 0:elec - full], orb[full:elec, :].astype(jnp.bfloat16),
        preferred_element_type=jnp.float32).astype(jnp.bfloat16)

    pl.semaphore_wait(barrier, line + jnp.where(is_end | is_helper, 1, 0))

    def copies(q, way, to):
        where = {"chol": to}
        first, last = buf.at[q, :, 0:cut], buf.at[q, :, cut:wide]
        return (
            pltpu.make_async_remote_copy(invb.at[q], invb.at[q], inv_send.at[way, q], inv_recv.at[q],
                                         device_id=where, device_id_type=MESH),
            pltpu.make_async_remote_copy(first, first, walk_send.at[way, 0, q], walk_recv.at[0, q],
                                         device_id=where, device_id_type=MESH),
            pltpu.make_async_remote_copy(last, last, walk_send.at[way, 1, q], walk_recv.at[1, q],
                                         device_id=where, device_id_type=MESH),
        )

    def ways(q, way, act):
        to = me + 1 - 2 * way
        inside = me < line - 1 if way == 0 else me > 0
        to_end = to == line - 1 if way == 0 else to == 0
        to = lax.rem(to + line, line)

        @pl.when(inside)
        def _():
            for copy in copies(q, way, to)[:2]:
                act(copy)

        @pl.when(inside & jnp.logical_not(to_end))
        def _():
            act(copies(q, way, to)[2])

    def send(q, way):
        ways(q, way, lambda copy: copy.start())

    def arrive(q):
        parts = copies(q, 0, lax.rem(me + 1, line))
        parts[0].wait_recv()
        parts[1].wait_recv()

        @pl.when(jnp.logical_not(is_end))
        def _():
            parts[2].wait_recv()

    def end_copies():
        where = {"chol": mate}
        return (
            pltpu.make_async_remote_copy(half_hbm.at[:, :, cut:basis], half_end, end_send.at[0], end_recv.at[0],
                                         device_id=where, device_id_type=MESH),
            pltpu.make_async_remote_copy(slab_hbm.at[:, cut:basis, :], slab_end, end_send.at[1], end_recv.at[1],
                                         device_id=where, device_id_type=MESH),
        )

    def bias_copy(at):
        return pltpu.make_async_remote_copy(fbv.at[at], fbo.at[at], fb_send.at[at], fb_recv.at[at],
                                            device_id={"spin": 1 - spin}, device_id_type=MESH)

    def mate_copies(at, q):
        return [pltpu.make_async_remote_copy(
            fbv.at[at], fbe.at[i, q], mate_send.at[i, q], mate_recv.at[i, q],
            device_id={"chol": mate, "spin": spin + i * (1 - 2 * spin)}, device_id_type=MESH) for i in range(2)]

    def update_copy(q):
        return pltpu.make_async_remote_copy(upd.at[q], acc.at[me], upd_send.at[q], upd_recv.at[me],
                                            device_id={"chol": q}, device_id_type=MESH)

    def contribution(q, x, left, g):
        met = lax.dot_general(x, left, NT, preferred_element_type=jnp.float32)
        part = jnp.sum(met[:, 0:lanes] * invb[q, 0:tall, :].astype(jnp.float32), axis=0, keepdims=True)
        part = jnp.sum(part, axis=1, keepdims=True)
        packed = invb[q, tall:tall + 32, :].astype(jnp.float32)
        for i in range(tall // 32):
            beside = met[32 * i:32 * i + 32, lanes:elec] * packed[:, rest * i:rest * i + rest]
            part = part + jnp.sum(jnp.sum(beside, axis=0, keepdims=True), axis=1, keepdims=True)
        return -part

    def own_vectors(q, size):
        for g in range(vectors):
            field = root_three * (aux_ref[g, q * walks + wx].astype(jnp.float32) - 1.0)
            field = jnp.where(spin == 0, field, 0.0)
            fbv[q, g:g + 1, :] = jnp.broadcast_to(
                field + contribution(q, buf[q, :, 0:size], half[g, :, 0:size], g), (1, rows))
        bias_copy(q).start()

        @pl.when(is_end & (q != me))
        def _():
            for copy in mate_copies(q, q):
                copy.start()
        for g in range(vectors):
            item[q, g] = jnp.dot(buf[q, :, 0:size], slab[g, 0:size, :], preferred_element_type=jnp.float32)

    def compute(q):
        partial = is_end & (q != me)

        @pl.when(partial)
        def _():
            own_vectors(q, cut)

        @pl.when(jnp.logical_not(partial))
        def _():
            own_vectors(q, basis)

    def compute_end(q):
        for g in range(vectors):
            fbv[line + q, g:g + 1, :] = jnp.broadcast_to(
                contribution(q, buf[q, :, cut:basis], half_end[g], g), (1, rows))
        bias_copy(line + q).start()
        for copy in mate_copies(line + q, q):
            copy.start()
        for g in range(vectors):
            item[line + q, g] = jnp.dot(buf[q, :, cut:basis], slab_end[g], preferred_element_type=jnp.float32)

    def mates_sum(q):
        for copy in mate_copies(q, q):
            copy.wait_recv()
        return fbe[0, q] + fbe[1, q]

    def weighted(at, shift):
        value = None
        for g in range(vectors):
            term = item[at, g] * (shift[g:g + 1, :] * scale)
            value = term if value is None else value + term
        return value

    def updated(q):
        bias_copy(q).wait_recv()

        @pl.when(is_end & (q != me))
        def _():
            fbo[q] = fbo[q] + mates_sum(q)
        total[...] = weighted(q, fbv[q] + fbo[q])

        @pl.when(is_helper & (q != mate))
        def _():
            bias_copy(line + q).wait_recv()
            total[...] += weighted(line + q, fbv[line + q] + fbo[line + q] + mates_sum(q))

    def give(q):
        updated(q)
        upd[q] = total[...].astype(jnp.bfloat16)
        update_copy(q).start()

    send(me, 0)
    send(me, 1)

    @pl.when(is_end)
    def _():
        for copy in end_copies():
            copy.start()
    loads[2].wait()
    loads[3].wait()
    fbv[...] = jnp.zeros_like(fbv)

    def level(d, carry):
        above, below = me + d, me - d

        @pl.when((above < line) & (d > 0))
        def _():
            arrive(above)
            send(above, 1)

        @pl.when((below >= 0) & (d > 0))
        def _():
            arrive(below)
            send(below, 0)

        def meet(side, carry):
            q = me + d - 2 * d * side

            @pl.when((q >= 0) & (q < line) & ((d > 0) | (side == 0)))
            def _():
                compute(q)
            return carry

        def now(side, carry):
            q = me + d - 2 * d * side

            @pl.when((q >= 0) & (q < line) & (d > 0) & jnp.logical_not(is_end | (is_helper & (q != mate))))
            def _():
                give(q)
            return carry

        lax.fori_loop(0, 2, meet, 0)
        lax.fori_loop(0, 2, now, 0)
        return carry

    lax.fori_loop(0, line, level, 0)

    @pl.when(is_helper)
    def _():
        for copy in end_copies():
            copy.wait_recv()

    def help_end(t, carry):
        d, side = t // 2, t % 2
        q = me + d - 2 * d * side

        @pl.when((q >= 0) & (q < line) & ((d > 0) | (side == 0)) & is_helper & (q != mate))
        def _():
            compute_end(q)
        return carry

    def late(t, carry):
        d, side = t // 2, t % 2
        q = me + d - 2 * d * side

        @pl.when((q >= 0) & (q < line) & (d > 0) & (is_end | (is_helper & (q != mate))))
        def _():
            give(q)
        return carry

    lax.fori_loop(0, 2 * line, help_end, 0)
    lax.fori_loop(2, 2 * line, late, 0)

    updated(me)
    res[...] = orb[:, 0:rows] - total[0:elec, :]
    for k in range(1, line):
        q = lax.rem(me + k, line)
        pltpu.make_async_remote_copy(upd.at[q], acc.at[q], upd_send.at[q], upd_recv.at[q],
                                     device_id={"chol": q}, device_id_type=MESH).wait_recv()
        res[...] -= acc[q].astype(jnp.float32)[0:elec, :]
    leave = pltpu.make_async_copy(res, out_hbm.at[:, 0, :], load_sem.at[0])
    leave.start()

    def drain(q, carry):
        @pl.when(q <= me)
        def _():
            ways(q, 0, lambda copy: copy.wait_send())

        @pl.when(q >= me)
        def _():
            ways(q, 1, lambda copy: copy.wait_send())

        bias_copy(q).wait_send()

        @pl.when(is_helper & (q != mate))
        def _():
            bias_copy(line + q).wait_send()

        @pl.when((is_end | is_helper) & (q != end))
        def _():
            for copy in mate_copies(q, q):
                copy.wait_send()

        @pl.when(q != me)
        def _():
            update_copy(q).wait_send()
        return carry

    lax.fori_loop(0, line, drain, 0)

    @pl.when(is_end)
    def _():
        for copy in end_copies():
            copy.wait_send()
    leave.wait()


def body(orbitals, intersection_inv, half_chol, slab_chol, aux_field):
    line = lax.axis_size("chol")
    walks = lax.axis_size("walk")
    basis, elec = orbitals.shape[2:]
    vectors, rows = slab_chol.shape[:2]
    tall, wide = up_to(elec, 32), up_to(basis, 128)
    cut = wide - 256
    bf16, f32 = jnp.bfloat16, jnp.float32
    dma = pltpu.SemaphoreType.DMA
    any_spec = pl.BlockSpec(memory_space=pl.ANY)
    out = pl.pallas_call(
        functools.partial(kernel, line, walks),
        out_shape=jax.ShapeDtypeStruct((elec, 1, rows), f32),
        in_specs=[any_spec] * 4 + [pl.BlockSpec(memory_space=pltpu.SMEM)],
        out_specs=any_spec,
        scratch_shapes=[
            pltpu.VMEM((elec, basis), f32),
            pltpu.VMEM((elec, elec), f32),
            pltpu.VMEM((vectors, elec, basis), bf16),
            pltpu.VMEM((vectors, basis, rows), bf16),
            pltpu.VMEM((vectors, elec, basis - cut), bf16),
            pltpu.VMEM((vectors, basis - cut, rows), bf16),
            pltpu.VMEM((elec, rows), f32),
            pltpu.VMEM((line, tall, wide), bf16),
            pltpu.VMEM((line, tall + 32, 128), bf16),
            pltpu.VMEM((2 * line, vectors, tall, rows), f32),
            pltpu.VMEM((2 * line, up_to(vectors, 8), rows), f32),
            pltpu.VMEM((2 * line, up_to(vectors, 8), rows), f32),
            pltpu.VMEM((2, line, up_to(vectors, 8), rows), f32),
            pltpu.VMEM((line, tall, rows), bf16),
            pltpu.VMEM((line, tall, rows), bf16),
            pltpu.VMEM((tall, rows), f32),
            dma((4,)),
            dma((2, 2, line)), dma((2, line)),
            dma((2, line)), dma((line,)),
            dma((2 * line,)), dma((2 * line,)),
            dma((2, line)), dma((2, line)),
            dma((line,)), dma((line,)),
            dma((2,)), dma((2,)),
        ],
        compiler_params=pltpu.CompilerParams(
            collective_id=0, has_side_effects=True, vmem_limit_bytes=63 * 1024 * 1024
        ),
    )(
        jnp.transpose(orbitals[0], (2, 0, 1)), jnp.transpose(intersection_inv[0], (1, 0, 2)),
        half_chol[:, 0], jnp.transpose(slab_chol, (0, 2, 1)), jnp.transpose(aux_field),
    )
    return jnp.transpose(out, (1, 2, 0))[None]


def solution(mesh):
    placed = (
        P(("groups", "chol", "walk"), "spin", None, None),
        P(("groups", "chol", "walk"), "spin", None, None),
        P("chol", "spin", None, None),
        P("chol", None, None),
        P("groups", "chol"),
    )
    return jax.shard_map(
        body,
        mesh=mesh,
        in_specs=placed,
        out_specs=P(("groups", "chol", "walk"), "spin", None, None),
        check_vma=False,
    )
```

```python
import functools
import math

import jax
import jax.numpy as jnp
from jax import lax
from jax.experimental import pallas as pl
from jax.experimental.pallas import tpu as pltpu
from jax.sharding import PartitionSpec as P

MESH = pl.DeviceIdType.MESH
root_three = math.sqrt(3.0)
NT = (((1,), (1,)), ((), ()))


def up_to(value, step):
    return -(-value // step) * step


def kernel(line, walks, orb_hbm, inv_hbm, half_hbm, slab_hbm, aux_ref, out_hbm,
           orb, inv, half, slab, half_end, slab_end, res, buf, invb, item, fbv, fbo, fbe, upd, acc, total, load_sem,
           walk_send, walk_recv, fb_send, fb_recv, mate_send, mate_recv, upd_send, upd_recv,
           end_send, end_recv):
    me = lax.axis_index("chol")
    spin = lax.axis_index("spin")
    wx = lax.axis_index("walk")
    elec, basis = orb.shape
    vectors = half.shape[0]
    rows = slab.shape[2]
    lanes = invb.shape[2]
    rest = elec - lanes
    tall, wide = buf.shape[1:]
    cut = basis - slab_end.shape[1]
    scale = 1.0 / math.sqrt(vectors * line)
    is_end = (me == 0) | (me == line - 1)
    is_helper = (me == 1) | (me == line - 2)
    mate = jnp.where(me == 0, 1, jnp.where(me == 1, 0, jnp.where(me == line - 1, line - 2, line - 1)))
    end = jnp.where(is_end, me, mate)

    loads = [pltpu.make_async_copy(src, dst, load_sem.at[i]) for i, (src, dst) in enumerate(
        ((orb_hbm.at[:, 0, :], orb), (inv_hbm.at[:, 0, :], inv), (half_hbm, half), (slab_hbm, slab)))]
    for load in loads:
        load.start()

    barrier = pltpu.get_barrier_semaphore()
    for k in range(1, line):
        pl.semaphore_signal(barrier, inc=1, device_id={"chol": lax.rem(me + k, line)}, device_id_type=MESH)
    pl.semaphore_signal(barrier, inc=1, device_id={"spin": 1 - spin}, device_id_type=MESH)


    @pl.when(is_end | is_helper)
    def _():
        pl.semaphore_signal(barrier, inc=1, device_id={"chol": mate, "spin": 1 - spin}, device_id_type=MESH)

    bounds = [0, 384, 768, cut, wide]
    eye = (lax.broadcasted_iota(jnp.int32, (tall, elec), 0)
           == lax.broadcasted_iota(jnp.int32, (tall, elec), 1)).astype(jnp.bfloat16)
    loads[1].wait()
    tall_inv = jnp.dot(eye, inv[...].astype(jnp.bfloat16), preferred_element_type=jnp.float32)
    invb[me, 0:tall, :] = tall_inv[:, 0:lanes].astype(jnp.bfloat16)
    side = [tall_inv[at:at + 32, lanes:elec] for at in range(0, tall, 32)]
    side.append(jnp.zeros((32, lanes - rest * len(side)), jnp.float32))
    invb[me, tall:tall + 32, :] = jnp.concatenate(side, axis=1).astype(jnp.bfloat16)
    full = elec // 16 * 16
    last = basis // 128 * 128
    buf[me, :, last:wide] = jnp.zeros((tall, wide - last), jnp.bfloat16)
    loads[0].wait()
    pl.semaphore_wait(barrier, line + jnp.where(is_end | is_helper, 1, 0))

    def piece(q, way, c, to):
        ref = invb.at[q] if c == 0 else buf.at[q, :, bounds[c - 1]:bounds[c]]
        return pltpu.make_async_remote_copy(ref, ref, walk_send.at[way, c, q], walk_recv.at[c, q],
                                            device_id={"chol": to}, device_id_type=MESH)

    def move(q, way, c, act):
        to = me + 1 - 2 * way
        inside = me < line - 1 if way == 0 else me > 0
        to_end = to == line - 1 if way == 0 else to == 0
        if c == len(bounds) - 1:
            inside = inside & jnp.logical_not(to_end)

        @pl.when(inside)
        def _():
            act(piece(q, way, c, lax.rem(to + line, line)))

    def arrive(q, way, c):
        wanted = jnp.logical_not(is_end) if c == len(bounds) - 1 else me >= 0

        @pl.when(wanted)
        def _():
            piece(q, 0, c, lax.rem(me + 1, line)).wait_recv()
            move(q, way, c, lambda copy: copy.start())

    def end_copies():
        where = {"chol": mate}
        return (
            pltpu.make_async_remote_copy(half_hbm.at[:, :, cut:basis], half_end, end_send.at[0], end_recv.at[0],
                                         device_id=where, device_id_type=MESH),
            pltpu.make_async_remote_copy(slab_hbm.at[:, cut:basis, :], slab_end, end_send.at[1], end_recv.at[1],
                                         device_id=where, device_id_type=MESH),
        )

    def bias_copy(at):
        return pltpu.make_async_remote_copy(fbv.at[at], fbo.at[at], fb_send.at[at], fb_recv.at[at],
                                            device_id={"spin": 1 - spin}, device_id_type=MESH)

    def mate_copies(at, q):
        return [pltpu.make_async_remote_copy(
            fbv.at[at], fbe.at[i, q], mate_send.at[i, q], mate_recv.at[i, q],
            device_id={"chol": mate, "spin": spin + i * (1 - 2 * spin)}, device_id_type=MESH) for i in range(2)]

    def update_copy(q):
        return pltpu.make_async_remote_copy(upd.at[q], acc.at[me], upd_send.at[q], upd_recv.at[me],
                                            device_id={"chol": q}, device_id_type=MESH)

    def contribution(q, x, left, g):
        met = lax.dot_general(x, left, NT, preferred_element_type=jnp.float32)
        part = jnp.sum(met[:, 0:lanes] * invb[q, 0:tall, :].astype(jnp.float32), axis=0, keepdims=True)
        part = jnp.sum(part, axis=1, keepdims=True)
        packed = invb[q, tall:tall + 32, :].astype(jnp.float32)
        for i in range(tall // 32):
            beside = met[32 * i:32 * i + 32, lanes:elec] * packed[:, rest * i:rest * i + rest]
            part = part + jnp.sum(jnp.sum(beside, axis=0, keepdims=True), axis=1, keepdims=True)
        return -part

    def own_vectors(q, size):
        for g in range(vectors):
            field = root_three * (aux_ref[g, q * walks + wx].astype(jnp.float32) - 1.0)
            field = jnp.where(spin == 0, field, 0.0)
            fbv[q, g:g + 1, :] = jnp.broadcast_to(
                field + contribution(q, buf[q, :, 0:size], half[g, :, 0:size], g), (1, rows))
        bias_copy(q).start()

        @pl.when(is_end & (q != me))
        def _():
            for copy in mate_copies(q, q):
                copy.start()
        for g in range(vectors):
            item[q, g] = jnp.dot(buf[q, :, 0:size], slab[g, 0:size, :], preferred_element_type=jnp.float32)

    def compute(q):
        partial = is_end & (q != me)

        @pl.when(partial)
        def _():
            own_vectors(q, cut)

        @pl.when(jnp.logical_not(partial))
        def _():
            own_vectors(q, basis)

    def compute_end(q):
        for g in range(vectors):
            fbv[line + q, g:g + 1, :] = jnp.broadcast_to(
                contribution(q, buf[q, :, cut:basis], half_end[g], g), (1, rows))
        bias_copy(line + q).start()
        for copy in mate_copies(line + q, q):
            copy.start()
        for g in range(vectors):
            item[line + q, g] = jnp.dot(buf[q, :, cut:basis], slab_end[g], preferred_element_type=jnp.float32)

    def mates_sum(q):
        for copy in mate_copies(q, q):
            copy.wait_recv()
        return fbe[0, q] + fbe[1, q]

    def weighted(at, shift):
        value = None
        for g in range(vectors):
            term = item[at, g] * (shift[g:g + 1, :] * scale)
            value = term if value is None else value + term
        return value

    def updated(q):
        bias_copy(q).wait_recv()

        @pl.when(is_end & (q != me))
        def _():
            fbo[q] = fbo[q] + mates_sum(q)
        total[...] = weighted(q, fbv[q] + fbo[q])

        @pl.when(is_helper & (q != mate))
        def _():
            bias_copy(line + q).wait_recv()
            total[...] += weighted(line + q, fbv[line + q] + fbo[line + q] + mates_sum(q))

    def give(q):
        updated(q)
        upd[q] = total[...].astype(jnp.bfloat16)
        update_copy(q).start()

    for c in range(len(bounds)):
        if c > 0:
            low, high = bounds[c - 1], min(bounds[c], basis)
            buf[me, 0:full, low:high] = orb[0:full, low:high].astype(jnp.bfloat16)
            buf[me, full:tall, low:high] = jnp.dot(
                eye[0:tall - full, 0:elec - full], orb[full:elec, low:high].astype(jnp.bfloat16),
                preferred_element_type=jnp.float32).astype(jnp.bfloat16)
        for way in range(2):
            move(me, way, c, lambda copy: copy.start())

    @pl.when(is_end)
    def _():
        for copy in end_copies():
            copy.start()
    loads[2].wait()
    loads[3].wait()
    fbv[...] = jnp.zeros_like(fbv)

    def level(d, carry):
        above, below = me + d, me - d

        for c in range(len(bounds)):
            @pl.when((above < line) & (d > 0))
            def _():
                arrive(above, 1, c)

            @pl.when((below >= 0) & (d > 0))
            def _():
                arrive(below, 0, c)

        def meet(side, carry):
            q = me + d - 2 * d * side

            @pl.when((q >= 0) & (q < line) & ((d > 0) | (side == 0)))
            def _():
                compute(q)
            return carry

        def now(side, carry):
            q = me + d - 2 * d * side

            @pl.when((q >= 0) & (q < line) & (d > 0) & jnp.logical_not(is_end | (is_helper & (q != mate))))
            def _():
                give(q)
            return carry

        lax.fori_loop(0, 2, meet, 0)
        lax.fori_loop(0, 2, now, 0)
        return carry

    lax.fori_loop(0, line, level, 0)

    @pl.when(is_helper)
    def _():
        for copy in end_copies():
            copy.wait_recv()

    def help_end(t, carry):
        d, side = t // 2, t % 2
        q = me + d - 2 * d * side

        @pl.when((q >= 0) & (q < line) & ((d > 0) | (side == 0)) & is_helper & (q != mate))
        def _():
            compute_end(q)
        return carry

    def late(t, carry):
        d, side = line - 1 - t // 2, t % 2
        q = me + d - 2 * d * side

        @pl.when((q >= 0) & (q < line) & (d > 0) & (is_end | (is_helper & (q != mate))))
        def _():
            give(q)
        return carry

    lax.fori_loop(0, 2 * line, help_end, 0)
    lax.fori_loop(0, 2 * line - 2, late, 0)

    updated(me)
    res[...] = orb[:, 0:rows] - total[0:elec, :]
    for k in range(1, line):
        q = lax.rem(me + k, line)
        pltpu.make_async_remote_copy(upd.at[q], acc.at[q], upd_send.at[q], upd_recv.at[q],
                                     device_id={"chol": q}, device_id_type=MESH).wait_recv()
        res[...] -= acc[q].astype(jnp.float32)[0:elec, :]
    leave = pltpu.make_async_copy(res, out_hbm.at[:, 0, :], load_sem.at[0])
    leave.start()

    def drain(q, carry):
        @pl.when(q <= me)
        def _():
            for c in range(len(bounds)):
                move(q, 0, c, lambda copy: copy.wait_send())

        @pl.when(q >= me)
        def _():
            for c in range(len(bounds)):
                move(q, 1, c, lambda copy: copy.wait_send())

        bias_copy(q).wait_send()

        @pl.when(is_helper & (q != mate))
        def _():
            bias_copy(line + q).wait_send()

        @pl.when((is_end | is_helper) & (q != end))
        def _():
            for copy in mate_copies(q, q):
                copy.wait_send()

        @pl.when(q != me)
        def _():
            update_copy(q).wait_send()
        return carry

    lax.fori_loop(0, line, drain, 0)

    @pl.when(is_end)
    def _():
        for copy in end_copies():
            copy.wait_send()
    leave.wait()


def body(orbitals, intersection_inv, half_chol, slab_chol, aux_field):
    line = lax.axis_size("chol")
    walks = lax.axis_size("walk")
    basis, elec = orbitals.shape[2:]
    vectors, rows = slab_chol.shape[:2]
    tall, wide = up_to(elec, 32), up_to(basis, 128)
    cut = wide - 256
    bf16, f32 = jnp.bfloat16, jnp.float32
    dma = pltpu.SemaphoreType.DMA
    any_spec = pl.BlockSpec(memory_space=pl.ANY)
    out = pl.pallas_call(
        functools.partial(kernel, line, walks),
        out_shape=jax.ShapeDtypeStruct((elec, 1, rows), f32),
        in_specs=[any_spec] * 4 + [pl.BlockSpec(memory_space=pltpu.SMEM)],
        out_specs=any_spec,
        scratch_shapes=[
            pltpu.VMEM((elec, basis), f32),
            pltpu.VMEM((elec, elec), f32),
            pltpu.VMEM((vectors, elec, basis), bf16),
            pltpu.VMEM((vectors, basis, rows), bf16),
            pltpu.VMEM((vectors, elec, basis - cut), bf16),
            pltpu.VMEM((vectors, basis - cut, rows), bf16),
            pltpu.VMEM((elec, rows), f32),
            pltpu.VMEM((line, tall, wide), bf16),
            pltpu.VMEM((line, tall + 32, 128), bf16),
            pltpu.VMEM((2 * line, vectors, tall, rows), f32),
            pltpu.VMEM((2 * line, up_to(vectors, 8), rows), f32),
            pltpu.VMEM((2 * line, up_to(vectors, 8), rows), f32),
            pltpu.VMEM((2, line, up_to(vectors, 8), rows), f32),
            pltpu.VMEM((line, tall, rows), bf16),
            pltpu.VMEM((line, tall, rows), bf16),
            pltpu.VMEM((tall, rows), f32),
            dma((4,)),
            dma((2, 5, line)), dma((5, line)),
            dma((2 * line,)), dma((2 * line,)),
            dma((2, line)), dma((2, line)),
            dma((line,)), dma((line,)),
            dma((2,)), dma((2,)),
        ],
        compiler_params=pltpu.CompilerParams(
            collective_id=0, has_side_effects=True, vmem_limit_bytes=63 * 1024 * 1024
        ),
    )(
        jnp.transpose(orbitals[0], (2, 0, 1)), jnp.transpose(intersection_inv[0], (1, 0, 2)),
        half_chol[:, 0], jnp.transpose(slab_chol, (0, 2, 1)), jnp.transpose(aux_field),
    )
    return jnp.transpose(out, (1, 2, 0))[None]


def solution(mesh):
    placed = (
        P(("groups", "chol", "walk"), "spin", None, None),
        P(("groups", "chol", "walk"), "spin", None, None),
        P("chol", "spin", None, None),
        P("chol", None, None),
        P("groups", "chol"),
    )
    return jax.shard_map(
        body,
        mesh=mesh,
        in_specs=placed,
        out_specs=P(("groups", "chol", "walk"), "spin", None, None),
        check_vma=False,
    )
```

```python
import functools
import math

import jax
import jax.numpy as jnp
from jax import lax
from jax.experimental import pallas as pl
from jax.experimental.pallas import tpu as pltpu
from jax.sharding import PartitionSpec as P

MESH = pl.DeviceIdType.MESH
root_three = math.sqrt(3.0)
NT = (((1,), (1,)), ((), ()))


def up_to(value, step):
    return -(-value // step) * step


def kernel(line, walks, orb_hbm, inv_hbm, half_hbm, slab_hbm, aux_ref, out_hbm,
           orb, inv, half, slab, half_end, slab_end, res, buf, invb, item, fbv, fbo, fbe, upd, acc, total, load_sem,
           walk_send, walk_recv, fb_send, fb_recv, mate_send, mate_recv, upd_send, upd_recv,
           end_send, end_recv):
    me = lax.axis_index("chol")
    spin = lax.axis_index("spin")
    wx = lax.axis_index("walk")
    elec, basis = orb.shape
    vectors = half.shape[0]
    rows = slab.shape[2]
    lanes = invb.shape[2]
    rest = elec - lanes
    tall, wide = buf.shape[1:]
    cut = basis - slab_end.shape[1]
    scale = 1.0 / math.sqrt(vectors * line)
    is_end = (me == 0) | (me == line - 1)
    is_helper = (me == 1) | (me == line - 2)
    mate = jnp.where(me == 0, 1, jnp.where(me == 1, 0, jnp.where(me == line - 1, line - 2, line - 1)))
    end = jnp.where(is_end, me, mate)

    loads = [pltpu.make_async_copy(src, dst, load_sem.at[i]) for i, (src, dst) in enumerate(
        ((orb_hbm.at[:, 0, :], orb), (inv_hbm.at[:, 0, :], inv), (half_hbm, half), (slab_hbm, slab)))]
    for load in loads:
        load.start()

    barrier = pltpu.get_barrier_semaphore()
    for k in range(1, line):
        pl.semaphore_signal(barrier, inc=1, device_id={"chol": lax.rem(me + k, line)}, device_id_type=MESH)
    pl.semaphore_signal(barrier, inc=1, device_id={"spin": 1 - spin}, device_id_type=MESH)


    @pl.when(is_end | is_helper)
    def _():
        pl.semaphore_signal(barrier, inc=1, device_id={"chol": mate, "spin": 1 - spin}, device_id_type=MESH)

    bounds = [0, 384, 768, cut, wide]
    eye = (lax.broadcasted_iota(jnp.int32, (tall, elec), 0)
           == lax.broadcasted_iota(jnp.int32, (tall, elec), 1)).astype(jnp.bfloat16)
    loads[1].wait()
    tall_inv = jnp.dot(eye, inv[...].astype(jnp.bfloat16), preferred_element_type=jnp.float32)
    invb[me, 0:tall, :] = tall_inv[:, 0:lanes].astype(jnp.bfloat16)
    side = [tall_inv[at:at + 32, lanes:elec] for at in range(0, tall, 32)]
    side.append(jnp.zeros((32, lanes - rest * len(side)), jnp.float32))
    invb[me, tall:tall + 32, :] = jnp.concatenate(side, axis=1).astype(jnp.bfloat16)
    full = elec // 16 * 16
    last = basis // 128 * 128
    buf[me, :, last:wide] = jnp.zeros((tall, wide - last), jnp.bfloat16)
    loads[0].wait()
    pl.semaphore_wait(barrier, line + jnp.where(is_end | is_helper, 1, 0))

    def piece(q, way, c, to):
        ref = invb.at[q] if c == 0 else buf.at[q, :, bounds[c - 1]:bounds[c]]
        return pltpu.make_async_remote_copy(ref, ref, walk_send.at[way, c, q], walk_recv.at[c, q],
                                            device_id={"chol": to}, device_id_type=MESH)

    def move(q, way, c, act):
        to = me + 1 - 2 * way
        inside = me < line - 1 if way == 0 else me > 0
        to_end = to == line - 1 if way == 0 else to == 0
        if c == len(bounds) - 1:
            inside = inside & jnp.logical_not(to_end)

        @pl.when(inside)
        def _():
            act(piece(q, way, c, lax.rem(to + line, line)))

    def arrive(q, way, c):
        wanted = jnp.logical_not(is_end) if c == len(bounds) - 1 else me >= 0

        @pl.when(wanted)
        def _():
            piece(q, 0, c, lax.rem(me + 1, line)).wait_recv()
            move(q, way, c, lambda copy: copy.start())

    share = pl.ds(pl.multiple_of(spin * (rows // 2), rows // 2), rows // 2)

    def end_copies():
        where = {"chol": mate}
        return (
            pltpu.make_async_remote_copy(half_hbm.at[:, :, cut:basis], half_end, end_send.at[0], end_recv.at[0],
                                         device_id=where, device_id_type=MESH),
            pltpu.make_async_remote_copy(slab_hbm.at[:, cut:basis, share], slab_end.at[:, :, share],
                                         end_send.at[1], end_recv.at[1], device_id=where, device_id_type=MESH),
        )

    def share_copy():
        return pltpu.make_async_remote_copy(slab_end.at[:, :, share], slab_end.at[:, :, share],
                                            end_send.at[2], end_recv.at[2],
                                            device_id={"spin": 1 - spin}, device_id_type=MESH)

    def bias_copy(at):
        return pltpu.make_async_remote_copy(fbv.at[at], fbo.at[at], fb_send.at[at], fb_recv.at[at],
                                            device_id={"spin": 1 - spin}, device_id_type=MESH)

    def mate_copies(at, q):
        return [pltpu.make_async_remote_copy(
            fbv.at[at], fbe.at[i, q], mate_send.at[i, q], mate_recv.at[i, q],
            device_id={"chol": mate, "spin": spin + i * (1 - 2 * spin)}, device_id_type=MESH) for i in range(2)]

    def update_copy(q):
        return pltpu.make_async_remote_copy(upd.at[q], acc.at[me], upd_send.at[q], upd_recv.at[me],
                                            device_id={"chol": q}, device_id_type=MESH)

    def contribution(q, x, left, g):
        met = lax.dot_general(x, left, NT, preferred_element_type=jnp.float32)
        part = jnp.sum(met[:, 0:lanes] * invb[q, 0:tall, :].astype(jnp.float32), axis=0, keepdims=True)
        part = jnp.sum(part, axis=1, keepdims=True)
        packed = invb[q, tall:tall + 32, :].astype(jnp.float32)
        for i in range(tall // 32):
            beside = met[32 * i:32 * i + 32, lanes:elec] * packed[:, rest * i:rest * i + rest]
            part = part + jnp.sum(jnp.sum(beside, axis=0, keepdims=True), axis=1, keepdims=True)
        return -part

    def own_vectors(q, size):
        for g in range(vectors):
            field = root_three * (aux_ref[g, q * walks + wx].astype(jnp.float32) - 1.0)
            field = jnp.where(spin == 0, field, 0.0)
            fbv[q, g:g + 1, :] = jnp.broadcast_to(
                field + contribution(q, buf[q, :, 0:size], half[g, :, 0:size], g), (1, rows))
        bias_copy(q).start()

        @pl.when(is_end & (q != me))
        def _():
            for copy in mate_copies(q, q):
                copy.start()
        for g in range(vectors):
            item[q, g] = jnp.dot(buf[q, :, 0:size], slab[g, 0:size, :], preferred_element_type=jnp.float32)

    def compute(q):
        partial = is_end & (q != me)

        @pl.when(partial)
        def _():
            own_vectors(q, cut)

        @pl.when(jnp.logical_not(partial))
        def _():
            own_vectors(q, basis)

    def compute_end(q):
        for g in range(vectors):
            fbv[line + q, g:g + 1, :] = jnp.broadcast_to(
                contribution(q, buf[q, :, cut:basis], half_end[g], g), (1, rows))
        bias_copy(line + q).start()
        for copy in mate_copies(line + q, q):
            copy.start()
        for g in range(vectors):
            item[line + q, g] = jnp.dot(buf[q, :, cut:basis], slab_end[g], preferred_element_type=jnp.float32)

    def mates_sum(q):
        for copy in mate_copies(q, q):
            copy.wait_recv()
        return fbe[0, q] + fbe[1, q]

    def weighted(at, shift):
        value = None
        for g in range(vectors):
            term = item[at, g] * (shift[g:g + 1, :] * scale)
            value = term if value is None else value + term
        return value

    def updated(q):
        bias_copy(q).wait_recv()

        @pl.when(is_end & (q != me))
        def _():
            fbo[q] = fbo[q] + mates_sum(q)
        total[...] = weighted(q, fbv[q] + fbo[q])

        @pl.when(is_helper & (q != mate))
        def _():
            bias_copy(line + q).wait_recv()
            total[...] += weighted(line + q, fbv[line + q] + fbo[line + q] + mates_sum(q))

    def give(q):
        updated(q)
        upd[q] = total[...].astype(jnp.bfloat16)
        update_copy(q).start()

    for c in range(len(bounds)):
        if c > 0:
            low, high = bounds[c - 1], min(bounds[c], basis)
            buf[me, 0:full, low:high] = orb[0:full, low:high].astype(jnp.bfloat16)
            buf[me, full:tall, low:high] = jnp.dot(
                eye[0:tall - full, 0:elec - full], orb[full:elec, low:high].astype(jnp.bfloat16),
                preferred_element_type=jnp.float32).astype(jnp.bfloat16)
        for way in range(2):
            move(me, way, c, lambda copy: copy.start())

    @pl.when(is_end)
    def _():
        for copy in end_copies():
            copy.start()
    loads[2].wait()
    loads[3].wait()
    fbv[...] = jnp.zeros_like(fbv)

    def level(d, carry):
        above, below = me + d, me - d

        for c in range(len(bounds)):
            @pl.when((above < line) & (d > 0))
            def _():
                arrive(above, 1, c)

            @pl.when((below >= 0) & (d > 0))
            def _():
                arrive(below, 0, c)

        def meet(side, carry):
            q = me + d - 2 * d * side

            @pl.when((q >= 0) & (q < line) & ((d > 0) | (side == 0)))
            def _():
                compute(q)
            return carry

        def now(side, carry):
            q = me + d - 2 * d * side

            @pl.when((q >= 0) & (q < line) & (d > 0) & jnp.logical_not(is_end | (is_helper & (q != mate))))
            def _():
                give(q)
            return carry

        lax.fori_loop(0, 2, meet, 0)
        lax.fori_loop(0, 2, now, 0)
        return carry

    lax.fori_loop(0, line, level, 0)

    @pl.when(is_helper)
    def _():
        first, second = end_copies()
        second.wait_recv()
        share_copy().start()
        first.wait_recv()
        share_copy().wait_recv()

    def help_end(t, carry):
        d, side = t // 2, t % 2
        q = me + d - 2 * d * side

        @pl.when((q >= 0) & (q < line) & ((d > 0) | (side == 0)) & is_helper & (q != mate))
        def _():
            compute_end(q)
        return carry

    def late(t, carry):
        d, side = line - 1 - t // 2, t % 2
        q = me + d - 2 * d * side

        @pl.when((q >= 0) & (q < line) & (d > 0) & (is_end | (is_helper & (q != mate))))
        def _():
            give(q)
        return carry

    lax.fori_loop(0, 2 * line, help_end, 0)
    lax.fori_loop(0, 2 * line - 2, late, 0)

    updated(me)
    res[...] = orb[:, 0:rows] - total[0:elec, :]
    for k in range(1, line):
        q = lax.rem(me + k, line)
        pltpu.make_async_remote_copy(upd.at[q], acc.at[q], upd_send.at[q], upd_recv.at[q],
                                     device_id={"chol": q}, device_id_type=MESH).wait_recv()
        res[...] -= acc[q].astype(jnp.float32)[0:elec, :]
    leave = pltpu.make_async_copy(res, out_hbm.at[:, 0, :], load_sem.at[0])
    leave.start()

    def drain(q, carry):
        @pl.when(q <= me)
        def _():
            for c in range(len(bounds)):
                move(q, 0, c, lambda copy: copy.wait_send())

        @pl.when(q >= me)
        def _():
            for c in range(len(bounds)):
                move(q, 1, c, lambda copy: copy.wait_send())

        bias_copy(q).wait_send()

        @pl.when(is_helper & (q != mate))
        def _():
            bias_copy(line + q).wait_send()

        @pl.when((is_end | is_helper) & (q != end))
        def _():
            for copy in mate_copies(q, q):
                copy.wait_send()

        @pl.when(q != me)
        def _():
            update_copy(q).wait_send()
        return carry

    lax.fori_loop(0, line, drain, 0)

    @pl.when(is_end)
    def _():
        for copy in end_copies():
            copy.wait_send()

    @pl.when(is_helper)
    def _():
        share_copy().wait_send()
    leave.wait()


def body(orbitals, intersection_inv, half_chol, slab_chol, aux_field):
    line = lax.axis_size("chol")
    walks = lax.axis_size("walk")
    basis, elec = orbitals.shape[2:]
    vectors, rows = slab_chol.shape[:2]
    tall, wide = up_to(elec, 32), up_to(basis, 128)
    cut = wide - 384
    bf16, f32 = jnp.bfloat16, jnp.float32
    dma = pltpu.SemaphoreType.DMA
    any_spec = pl.BlockSpec(memory_space=pl.ANY)
    out = pl.pallas_call(
        functools.partial(kernel, line, walks),
        out_shape=jax.ShapeDtypeStruct((elec, 1, rows), f32),
        in_specs=[any_spec] * 4 + [pl.BlockSpec(memory_space=pltpu.SMEM)],
        out_specs=any_spec,
        scratch_shapes=[
            pltpu.VMEM((elec, basis), f32),
            pltpu.VMEM((elec, elec), f32),
            pltpu.VMEM((vectors, elec, basis), bf16),
            pltpu.VMEM((vectors, basis, rows), bf16),
            pltpu.VMEM((vectors, elec, basis - cut), bf16),
            pltpu.VMEM((vectors, basis - cut, rows), bf16),
            pltpu.VMEM((elec, rows), f32),
            pltpu.VMEM((line, tall, wide), bf16),
            pltpu.VMEM((line, tall + 32, 128), bf16),
            pltpu.VMEM((2 * line, vectors, tall, rows), f32),
            pltpu.VMEM((2 * line, up_to(vectors, 8), rows), f32),
            pltpu.VMEM((2 * line, up_to(vectors, 8), rows), f32),
            pltpu.VMEM((2, line, up_to(vectors, 8), rows), f32),
            pltpu.VMEM((line, tall, rows), bf16),
            pltpu.VMEM((line, tall, rows), bf16),
            pltpu.VMEM((tall, rows), f32),
            dma((4,)),
            dma((2, 5, line)), dma((5, line)),
            dma((2 * line,)), dma((2 * line,)),
            dma((2, line)), dma((2, line)),
            dma((line,)), dma((line,)),
            dma((3,)), dma((3,)),
        ],
        compiler_params=pltpu.CompilerParams(
            collective_id=0, has_side_effects=True, vmem_limit_bytes=63 * 1024 * 1024
        ),
    )(
        jnp.transpose(orbitals[0], (2, 0, 1)), jnp.transpose(intersection_inv[0], (1, 0, 2)),
        half_chol[:, 0], jnp.transpose(slab_chol, (0, 2, 1)), jnp.transpose(aux_field),
    )
    return jnp.transpose(out, (1, 2, 0))[None]


def solution(mesh):
    placed = (
        P(("groups", "chol", "walk"), "spin", None, None),
        P(("groups", "chol", "walk"), "spin", None, None),
        P("chol", "spin", None, None),
        P("chol", None, None),
        P("groups", "chol"),
    )
    return jax.shard_map(
        body,
        mesh=mesh,
        in_specs=placed,
        out_specs=P(("groups", "chol", "walk"), "spin", None, None),
        check_vma=False,
    )
```
